32 devices in a mesh: gx: 4 (over y, x), gy: 8 (over z, core).
Axes of the slice: x: 2, y: 2, z: 4, core: 2. Of those that a mesh axis runs over, the one named last changes fastest.
Arguments:
- rhs_base: float32 [8, 64, 1024], P(None, 'gx', 'gy'), may hold values from -12 to 12
- cond_base: float32 [8, 64, 1024], P(None, 'gx', 'gy'), may hold values from 0.1 to 1
- cap_base: float32 [8, 64, 1024], P(None, 'gx', 'gy'), may hold values from 0.02 to 0.5
- patch_rhs: float32 [512, 8, 256], P(('gx', 'gy')), may hold values from -12 to 12
- patch_cond: float32 [512, 8, 256], P(('gx', 'gy')), may hold values from 0.1 to 1
- patch_cap: float32 [512, 8, 256], P(('gx', 'gy')), may hold values from 0.02 to 0.5
- box_list: int32 [1024, 2], P(('gx', 'gy')), may hold values from -1 to 31, as said below
- patch_from: int32 [512], P(('gx', 'gy')), may hold values from 0 to 31, as said below
Outputs:
- solution_field: float32 [8, 64, 1024], P(None, 'gx', 'gy')
- patch_field: float32 [512, 8, 256], P(('gx', 'gy'))
The draws below stay inside these ranges and needn't reach their ends.
Inputs may be any that keep to these rules, and one draw needn't show every extreme that they name: `box_list`: rows (a 8 + b) * 32 to (a 8 + b + 1) * 32 - 1 are tile (a, b)'s boxes: column 0 a footprint slot, column 1 the send row o * 4 + c for its c-th box to owner (a, o). Used entries come first, unused ones hold -1 in both columns; slots and send rows are distinct within a tile; each owner receives exactly 16 boxes in all. `patch_from`: entry (a 8 + o) * 16 + j is s * 4 + c for the box of tile (a, s) with send row o * 4 + c; the 16 entries of one device are distinct.
All inputs are finite; a program needn't handle non-finite values.
Results may differ from the reference program's by a relative error of at most 0.0001.
Values sent between devices are 32-bit elements; how exact they have to be, the bound alone decides.
A program may use at most 128 MiB of HBM per device.

```python
import math
import jax
import jax.numpy as jnp
from jax import lax

NZ = 8
CX = 16
CY = 128
SWEEPS = 12
PS = 16
CAP = 4
BOXES = 32
PATCHES = 512
NX = 64
NY = 1024
N_GX = 4
N_GY = 8


def plan_tables(key):
    base_key = jax.random.fold_in(key, 4242)
    half_count = N_GY // 2
    row_count = N_GY * CAP

    def single_row(row_key, row_index):
        key_perm, key_skew, key_slot, key_rank = jax.random.split(row_key, 4)
        tile_ids = jnp.arange(N_GY, dtype=jnp.int32)
        shuffled = jax.random.permutation(key_perm, N_GY).astype(jnp.int32)
        target = jnp.where(row_index == 0, 0, jnp.where(row_index == 1, N_GY - 1, shuffled[0])).astype(jnp.int32)
        shuffled = jnp.where(shuffled == target, shuffled[0], jnp.where(tile_ids == 0, target, shuffled))
        imbalance = jax.random.randint(key_skew, (half_count,), 0, half_count + 1).astype(jnp.int32).at[0].set(half_count)
        tile_loads = jnp.zeros((N_GY,), jnp.int32).at[shuffled[0::2]].set(half_count + imbalance).at[shuffled[1::2]].set(half_count - imbalance)
        window_start = (jnp.cumsum(tile_loads) - tile_loads) % N_GY
        entry_ids = jnp.arange(BOXES, dtype=jnp.int32)
        window_step = entry_ids // CAP
        lane_ids = entry_ids % CAP
        is_used = window_step[None, :] < tile_loads[:, None]
        owner_ids = (window_start[:, None] + window_step[None, :]) % N_GY
        send_rows = owner_ids * CAP + lane_ids[None, :]

        def slot_order(slot_key):
            return jax.random.permutation(slot_key, BOXES).astype(jnp.int32)
        slot_ids = jax.vmap(slot_order)(jax.random.split(key_slot, N_GY))
        box_rows = jnp.stack([jnp.where(is_used, slot_ids, -1), jnp.where(is_used, send_rows, -1)], axis=-1)
        offset = (tile_ids[:, None] - window_start[None, :]) % N_GY
        covered = offset < tile_loads[None, :]
        row_ids = jnp.arange(row_count, dtype=jnp.int32)
        is_live = covered[:, row_ids // CAP]

        def rank_order(rank_key):
            return jax.random.permutation(rank_key, row_count).astype(jnp.int32)
        random_rank = jax.vmap(rank_order)(jax.random.split(key_rank, N_GY))
        sort_score = jnp.where(is_live, random_rank, random_rank + row_count)
        received = jnp.argsort(sort_score, axis=1)[:, :PS].astype(jnp.int32)
        return (box_rows, received)
    row_keys = jax.random.split(base_key, N_GX)
    box_rows, received = jax.vmap(single_row)(row_keys, jnp.arange(N_GX, dtype=jnp.int32))
    return (box_rows.reshape(N_GX * N_GY * BOXES, 2).astype(jnp.int32), received.reshape(-1).astype(jnp.int32))


def draw_box_list(key, part):
    return plan_tables(key)[0]


def draw_patch_from(key, part):
    return plan_tables(key)[1]


def draw_rhs_base(key, part):
    noise_key = jax.random.fold_in(key, 7717)
    extent = (NZ, NX, NY)
    rough = 2.0 * jax.random.normal(noise_key, extent, jnp.float32)
    return jnp.clip(rough, -12.0, 12.0).astype(jnp.float32)


def block_scale(key, shape, cuts, low, high):
    gain, own = 1.0, jax.random.fold_in(key, 6)
    for dim, shards_of in cuts:
        heights = jnp.exp(jax.random.uniform(jax.random.fold_in(own, dim), (shards_of,), jnp.float32, low / len(cuts), high / len(cuts)))
        gain = gain * jnp.repeat(heights, shape[dim] // shards_of).reshape([-1 if axis == dim else 1 for axis in range(len(shape))])
    return gain


def bell_draw(own_key, shape, spread, bound, cuts=(), kind=jnp.bfloat16):
    values = spread * jax.random.normal(own_key, shape, jnp.float32)
    if cuts:
        values = values * block_scale(own_key, shape, cuts, -0.22, 0.18)
    return jnp.clip(values, -bound, bound).astype(kind)


def setup_inputs(seed: int = 0) -> dict:
    key_of = jax.random.split(jax.random.key(seed), 9)
    return {
        "rhs_base": draw_rhs_base(jax.random.fold_in(key_of[8], 71), 0),
        "cond_base": jnp.clip(jnp.exp(math.log(1.0) - 2.3025851 * jax.random.uniform(key_of[1], (NZ, NX, NY), jnp.float32) ** block_scale(key_of[1], (NZ, NX, NY), ((1, 4), (2, 8)), -0.2, 0.2)), 0.1, 1.0),
        "cap_base": jnp.clip(jnp.exp(math.log(0.5) - 3.218876 * jax.random.uniform(key_of[2], (NZ, NX, NY), jnp.float32) ** block_scale(key_of[2], (NZ, NX, NY), ((1, 4), (2, 8)), -0.2, 0.2)), 0.02, 0.5),
        "patch_rhs": bell_draw(key_of[3], (PATCHES, NZ, 256), 2.0, 12.0, ((0, 32),), jnp.float32),
        "patch_cond": jnp.clip(jnp.exp(math.log(1.0) - 2.3025851 * jax.random.uniform(key_of[4], (PATCHES, NZ, 256), jnp.float32) ** block_scale(key_of[4], (PATCHES, NZ, 256), ((0, 32),), -0.2, 0.2)), 0.1, 1.0),
        "patch_cap": jnp.clip(jnp.exp(math.log(0.5) - 3.218876 * jax.random.uniform(key_of[5], (PATCHES, NZ, 256), jnp.float32) ** block_scale(key_of[5], (PATCHES, NZ, 256), ((0, 32),), -0.2, 0.2)), 0.02, 0.5),
        "box_list": draw_box_list(jax.random.fold_in(key_of[8], 71), 0),
        "patch_from": draw_patch_from(jax.random.fold_in(key_of[8], 71), 0),
    }


RELAX = 0.8
LATERAL = 16.0
DEPTH_WEIGHT = 1.0
PATCH_WEIGHT = 64.0


def layered(values, layer_axis):
    layer_count = values.shape[layer_axis]
    beneath = jnp.concatenate([lax.slice_in_dim(values, 0, 1, axis=layer_axis), lax.slice_in_dim(values, 0, layer_count - 1, axis=layer_axis)], axis=layer_axis)
    overhead = jnp.concatenate([lax.slice_in_dim(values, 1, layer_count, axis=layer_axis), lax.slice_in_dim(values, layer_count - 1, layer_count, axis=layer_axis)], axis=layer_axis)
    return beneath, overhead


def coefficients(conduct_pad, capacity, weight):
    conduct = conduct_pad[..., 1:-1, 1:-1]
    layer_axis = conduct.ndim - 3
    flux_west = 0.5 * weight * (conduct + conduct_pad[..., :-2, 1:-1])
    flux_east = 0.5 * weight * (conduct + conduct_pad[..., 2:, 1:-1])
    flux_south = 0.5 * weight * (conduct + conduct_pad[..., 1:-1, :-2])
    flux_north = 0.5 * weight * (conduct + conduct_pad[..., 1:-1, 2:])
    beneath, overhead = layered(conduct, layer_axis)
    layer_index = lax.broadcasted_iota(jnp.int32, conduct.shape, layer_axis)
    layer_count = conduct.shape[layer_axis]
    flux_below = jnp.where(layer_index > 0, 0.5 * DEPTH_WEIGHT * (conduct + beneath), 0.0)
    flux_above = jnp.where(layer_index < layer_count - 1, 0.5 * DEPTH_WEIGHT * (conduct + overhead), 0.0)
    diagonal = capacity + flux_west + flux_east + flux_south + flux_north + flux_below + flux_above
    return (flux_west, flux_east, flux_south, flux_north, flux_below, flux_above, capacity, diagonal)


def operate(padded, stencil):
    values = padded[..., 1:-1, 1:-1]
    beneath, overhead = layered(values, values.ndim - 3)
    return (stencil[6] * values + stencil[0] * (values - padded[..., :-2, 1:-1]) + stencil[1] * (values - padded[..., 2:, 1:-1])
            + stencil[2] * (values - padded[..., 1:-1, :-2]) + stencil[3] * (values - padded[..., 1:-1, 2:])
            + stencil[4] * (values - beneath) + stencil[5] * (values - overhead))


def sweep(padded, source, stencil):
    values = padded[..., 1:-1, 1:-1]
    return values + RELAX * (source - operate(padded, stencil)) / stencil[7]


def pad_zero(values):
    return jnp.pad(values, ((0, 0), (1, 1), (1, 1)))


def coarsen(values):
    dims_in = values.shape
    split_view = values.reshape(dims_in[:-2] + (dims_in[-2] // 2, 2, dims_in[-1] // 2, 2))
    return 0.25 * jnp.sum(split_view, axis=(-3, -1))


def refine(values):
    return jnp.repeat(jnp.repeat(values, 2, axis=-2), 2, axis=-1)


def cut_window(padded, row_start, col_start):
    window_block = lax.dynamic_slice(padded, (row_start * 0, row_start, col_start), (padded.shape[0], 10, 10))
    footprint = window_block[:, 1:9, 1:9].reshape(padded.shape[0], 64)
    return jnp.concatenate([footprint, window_block[:, 0, 1:9], window_block[:, 9, 1:9], window_block[:, 1:9, 0], window_block[:, 1:9, 9]], axis=-1)


def ghosted(values, window):
    padded = jnp.pad(values, ((0, 0), (0, 0), (1, 1), (1, 1)))
    padded = padded.at[..., 0, 1:-1].set(jnp.repeat(window[..., 64:72], 2, axis=-1))
    padded = padded.at[..., -1, 1:-1].set(jnp.repeat(window[..., 72:80], 2, axis=-1))
    padded = padded.at[..., 1:-1, 0].set(jnp.repeat(window[..., 80:88], 2, axis=-1))
    padded = padded.at[..., 1:-1, -1].set(jnp.repeat(window[..., 88:96], 2, axis=-1))
    return padded


def cycle_from(level_index, source, stencils):
    stencil = stencils[level_index]
    values = RELAX * source / stencil[7]
    if level_index == 3:
        for sweep_index in range(SWEEPS - 1):
            values = sweep(pad_zero(values), source, stencil)
        return values
    values = sweep(pad_zero(values), source, stencil)
    residual = source - operate(pad_zero(values), stencil)
    values = values + refine(cycle_from(level_index + 1, coarsen(residual), stencils))
    return sweep(pad_zero(values), source, stencil)


def reference(rhs_base, cond_base, cap_base, patch_rhs, patch_cond, patch_cap, box_list, patch_from):
    stencils = []
    conduct, capacity, weight = cond_base, cap_base, LATERAL
    for level_index in range(4):
        stencils.append(coefficients(pad_zero(conduct), capacity, weight))
        if level_index < 3:
            conduct, capacity, weight = coarsen(conduct), coarsen(capacity), weight / 4.0
    lane_count = 2 * PS
    box_rows = box_list.reshape(N_GX, N_GY, BOXES, 2)
    slot_ids = box_rows[..., 0]
    send_rows = box_rows[..., 1]
    tile_x = jnp.broadcast_to(jnp.arange(N_GX, dtype=jnp.int32)[:, None, None], send_rows.shape)
    tile_y = jnp.broadcast_to(jnp.arange(N_GY, dtype=jnp.int32)[None, :, None], send_rows.shape)
    slot_table = jnp.full((N_GX, N_GY, lane_count + 1), -1, jnp.int32)
    slot_table = slot_table.at[tile_x, tile_y, jnp.where(send_rows >= 0, send_rows, lane_count)].set(slot_ids)
    incoming = patch_from.reshape(N_GX, N_GY, PS)
    source_tile = incoming // CAP
    lane_ids = incoming % CAP
    owner_ids = jnp.arange(N_GY, dtype=jnp.int32)[None, :, None]
    row_x = jnp.arange(N_GX, dtype=jnp.int32)[:, None, None]
    patch_slot = slot_table[row_x, source_tile, owner_ids * CAP + lane_ids]
    anchor_x = (row_x * CX + 8 * (patch_slot // (CY // 8))).reshape(-1).astype(jnp.int32)
    anchor_y = (source_tile * CY + 8 * (patch_slot % (CY // 8))).reshape(-1).astype(jnp.int32)

    base_stencil = stencils[0]
    values = RELAX * rhs_base / base_stencil[7]
    values = sweep(pad_zero(values), rhs_base, base_stencil)
    padded = pad_zero(values)

    def windows_of(grid_padded):
        def single(row_start, col_start):
            return cut_window(grid_padded, row_start, col_start)
        return jax.vmap(single)(anchor_x, anchor_y)

    first_window = windows_of(padded)
    patch_conduct = patch_cond.reshape(PATCHES, NZ, 16, 16)
    patch_stencil = coefficients(jnp.pad(patch_conduct, ((0, 0), (0, 0), (1, 1), (1, 1)), mode="edge"), patch_cap.reshape(PATCHES, NZ, 16, 16), PATCH_WEIGHT)
    patch_source = patch_rhs.reshape(PATCHES, NZ, 16, 16)
    patch_values = jnp.zeros((PATCHES, NZ, 16, 16), jnp.float32)
    for sweep_index in range(2):
        patch_values = sweep(ghosted(patch_values, first_window), patch_source, patch_stencil)
    restricted = coarsen(patch_source - operate(ghosted(patch_values, first_window), patch_stencil))
    residual = rhs_base - operate(padded, base_stencil)
    offsets = jnp.arange(8, dtype=jnp.int32)
    index_x = anchor_x[:, None, None] + offsets[None, :, None] + 0 * offsets[None, None, :]
    index_y = anchor_y[:, None, None] + offsets[None, None, :] + 0 * offsets[None, :, None]
    residual = residual.at[:, index_x, index_y].set(jnp.transpose(restricted, (1, 0, 2, 3)))
    corrected = values + refine(cycle_from(1, coarsen(residual), stencils))
    smoothed = sweep(pad_zero(corrected), rhs_base, base_stencil)
    second_window = windows_of(pad_zero(smoothed))
    change = refine((second_window[..., :64] - first_window[..., :64]).reshape(PATCHES, NZ, 8, 8))
    patch_values = patch_values + change
    patch_values = sweep(ghosted(patch_values, second_window), patch_source, patch_stencil)
    return smoothed, patch_values.reshape(PATCHES, NZ, 256)
```

```python
import functools
import jax
import jax.numpy as jnp
from jax import lax
from jax.experimental import pallas as pl
from jax.experimental.pallas import tpu as pltpu
from jax.sharding import PartitionSpec as P

SWEEPS = 12
RELAX = 0.8
F32 = jnp.float32
HALO = 4
MESH = pl.DeviceIdType.MESH


def table(rows, cols, rule):
    src = lax.broadcasted_iota(jnp.int32, (rows, cols), 0)
    dst = lax.broadcasted_iota(jnp.int32, (rows, cols), 1)
    return rule(src, dst).astype(jnp.bfloat16)


def apply_table(values, matrix):
    lead = values.shape[:-1]
    flat = values.reshape(-1, values.shape[-1])
    high = flat.astype(jnp.bfloat16)
    low = (flat - high.astype(F32)).astype(jnp.bfloat16)
    out = jnp.dot(high, matrix, preferred_element_type=F32) + jnp.dot(
        low, matrix, preferred_element_type=F32
    )
    return out.reshape(lead + (matrix.shape[1],))


def lanes(values, shift):
    return pltpu.roll(values, shift % values.shape[-1], values.ndim - 1)


def layers(values, shift):
    return pltpu.roll(values, shift % 8, values.ndim - 2)


def rows_up(values):
    return jnp.concatenate([values[1:], jnp.zeros_like(values[:1])], axis=0)


def rows_down(values):
    return jnp.concatenate([jnp.zeros_like(values[:1]), values[:-1]], axis=0)


def stencil_of(conduct, capacity, weight, mask):
    half = 0.5 * weight
    layer = lax.broadcasted_iota(jnp.int32, conduct.shape, 1)
    east = half * (conduct + rows_up(conduct))
    west = half * (conduct + rows_down(conduct))
    north = half * (conduct + lanes(conduct, -1))
    above = jnp.where(layer < 7, 0.5 * (conduct + layers(conduct, -1)), 0.0)
    diagonal = (
        capacity + east + west + north + lanes(north, 1) + above + layers(above, 1)
    )
    gain = jnp.where(mask, RELAX / diagonal, 0.0)
    return (east, west, north, above, diagonal, gain)


def around(values, stencil):
    east, west, north, above, _, _ = stencil
    return (
        east * rows_up(values)
        + west * rows_down(values)
        + north * lanes(values, -1)
        + lanes(north * values, 1)
        + above * layers(values, -1)
        + layers(above * values, 1)
    )


def smooth(values, source, stencil):
    return (1.0 - RELAX) * values + stencil[5] * (source + around(values, stencil))


def residual_of(values, source, stencil):
    return source - stencil[4] * values + around(values, stencil)


def pair_rows(values):
    count = values.shape[0] // 2
    split = values.reshape((count, 2) + values.shape[1:])
    return split[:, 0] + split[:, 1]


def repeat_rows(values):
    count = values.shape[0]
    return jnp.broadcast_to(values[:, None], (count, 2) + values.shape[1:]).reshape(
        (2 * count,) + values.shape[1:]
    )


def exchange_groups(items):
    group = lax.broadcasted_iota(jnp.int32, (8, 128), 1) // 8
    turned = [items[(-n) % 16] for n in range(16)]
    turned = [lanes(v, 8 * ((-n) % 16)) if n else v for n, v in enumerate(turned)]
    for bit in range(4):
        step = 1 << bit
        picked = (group // step) % 2 == 1
        turned = [jnp.where(picked, turned[(n - step) % 16], turned[n]) for n in range(16)]
    return [lanes(v, -8 * n) if n else v for n, v in enumerate(turned)]


def windows_into(field, out_ref):
    lane = lax.broadcasted_iota(jnp.int32, (8, 128), 1)
    for band in range(2):
        first = HALO + 8 * band
        items = [field[first + i, :, :128] for i in range(8)]
        south = jnp.zeros((8, 128), F32)
        north = jnp.zeros((8, 128), F32)
        for i in range(8):
            edge = jnp.where((lane == 0) | (lane == 127), field[first + i, :, 128:], items[i])
            south = jnp.where(lane % 8 == i, lanes(edge, i + 1), south)
            north = jnp.where(lane % 8 == i, lanes(edge, i - 8), north)
        items = items + [field[first - 1, :, :128], field[first + 8, :, :128], south, north]
        items = items + [jnp.zeros((8, 128), F32)] * 4
        for col, window in enumerate(exchange_groups(items)):
            out_ref[16 * band + col] = window


def kernel(
    n_gx, n_gy, cap_rows, tables, froms,
    rhs_ref, cond_ref, capb_ref, prhs_ref, pcond_ref, pcap_ref,
    field_ref, patch_ref,
    tile, side, from_rows, from_side, from_corner,
    slots, out1, in1, out2, in2, out3, in3, win1, win2, rest,
    coarse_k, coarse_g, column,
    send_a, recv_a, send_x, recv_x, send_k, recv_k, send_g, recv_g,
):
    a = lax.axis_index("gx")
    b = lax.axis_index("gy")
    has_up, has_down = a > 0, a < n_gx - 1
    has_left, has_right = b > 0, b < n_gy - 1
    ok_gx = {-1: has_up, 0: None, 1: has_down}
    ok_gy = {-1: has_left, 0: None, 1: has_right}

    def guarded(cond, action):
        if cond is None:
            action()
        else:
            pl.when(cond)(action)

    barrier = pltpu.get_barrier_semaphore()

    def greet(x, y):
        pl.semaphore_signal(barrier, inc=1, device_id=(x, y), device_id_type=MESH)

    for d in range(1, n_gy):
        greet(a, lax.rem(b + d, n_gy))
    for d in range(1, n_gx):
        for dy in (-1, 0, 1):
            guarded(ok_gy[dy], lambda d=d, dy=dy: greet(lax.rem(a + d, n_gx), b + dy))
    columns = 1 + has_left.astype(jnp.int32) + has_right.astype(jnp.int32)

    lane = lax.broadcasted_iota(jnp.int32, (8, 128), 1)
    own = []
    for index, ref in enumerate((cond_ref, capb_ref, rhs_ref)):
        rows = [ref[pl.ds(x, 8, stride=16), :] for x in range(16)]
        for x in range(16):
            tile[index, x] = rows[x]
        for part in range(2):
            packed = lanes(rows[8 * part], 8)
            for i in range(1, 8):
                packed = jnp.where(lane // 16 == i, lanes(rows[8 * part + i], 8 + 16 * i), packed)
            side[part, index] = packed
        own.append(jnp.stack(rows))

    pl.semaphore_wait(barrier, n_gy - 1 + (n_gx - 1) * columns)

    def start_wait(copies):
        for cond, make in copies:
            guarded(cond, lambda make=make: make().start())

    def wait_recv(copies):
        for cond, make in copies:
            guarded(cond, lambda make=make: make().wait_recv())

    def wait_send(copies):
        for cond, make in copies:
            guarded(cond, lambda make=make: make().wait_send())

    def remote(src, dst, ssem, rsem, x, y):
        return pltpu.make_async_remote_copy(
            src_ref=src, dst_ref=dst, send_sem=ssem, recv_sem=rsem,
            device_id=(x, y), device_id_type=MESH,
        )

    halo_send, halo_recv = [], []
    for dx in (-1, 0, 1):
        for dy in (-1, 0, 1):
            if dx == 0 and dy == 0:
                continue
            conds = [c for c in (ok_gx[dx], ok_gy[dy]) if c is not None]
            cond = conds[0] if len(conds) == 1 else jnp.logical_and(conds[0], conds[1])
            place = 3 * (dx + 1) + dy + 1
            back = 3 * (1 - dx) + 1 - dy

            def views(dx=dx, dy=dy):
                if dy == 0:
                    start = 0 if dx < 0 else 16 - HALO
                    return tile.at[:, pl.ds(start, HALO)], from_rows.at[(1 - dx) // 2]
                if dx == 0:
                    return side, from_side.at[(1 - dy) // 2]
                part = 0 if dx < 0 else 1
                return side.at[part], from_corner.at[(1 - dx) // 2, (1 - dy) // 2]

            def landing(dx=dx, dy=dy):
                if dy == 0:
                    return from_rows.at[(1 + dx) // 2]
                if dx == 0:
                    return from_side.at[(1 + dy) // 2]
                return from_corner.at[(1 + dx) // 2, (1 + dy) // 2]

            def out(views=views, dx=dx, dy=dy, place=place, back=back):
                src, dst = views()
                return remote(src, dst, send_a.at[place], recv_a.at[back], a + dx, b + dy)

            def arrive(landing=landing, dx=dx, dy=dy, place=place):
                return remote(landing(), landing(), send_a.at[place], recv_a.at[place], a + dx, b + dy)

            halo_send.append((cond, out))
            halo_recv.append((cond, arrive))
    start_wait(halo_send)

    def all_to_all(phase, src, dst):
        sends, recvs = [], []
        for d in range(1, n_gy):
            def out(d=d):
                to = lax.rem(b + d, n_gy)
                return remote(
                    src.at[pl.ds(to * cap_rows, cap_rows)], dst.at[pl.ds(b * cap_rows, cap_rows)],
                    send_x.at[phase, d], recv_x.at[phase, d], a, to,
                )

            def arrive(d=d):
                at = lax.rem(b + n_gy - d, n_gy)
                piece = dst.at[pl.ds(at * cap_rows, cap_rows)]
                return remote(piece, piece, send_x.at[phase, d], recv_x.at[phase, d], a, at)

            sends.append((None, out))
            recvs.append((None, arrive))
        start_wait(sends)
        mine = pl.ds(b * cap_rows, cap_rows)
        dst[mine] = src[mine]
        return sends, recvs

    def gather(buffer, ssem, rsem):
        sends, recvs = [], []
        for dy in (0, -1, 1):
            for d in range(n_gx):
                if dy == 0 and d == 0:
                    continue

                def out(d=d, dy=dy):
                    to = lax.rem(a + d, n_gx)
                    return remote(
                        buffer.at[1, a], buffer.at[1 - dy, a],
                        ssem.at[dy + 1, d], rsem.at[1 - dy, d], to, b + dy,
                    )

                def arrive(d=d, dy=dy):
                    at = lax.rem(a + n_gx - d, n_gx)
                    piece = buffer.at[dy + 1, at]
                    return remote(piece, piece, ssem.at[dy + 1, d], rsem.at[dy + 1, d], at, b + dy)

                sends.append((ok_gy[dy], out))
                recvs.append((ok_gy[dy], arrive))
        start_wait(sends)
        return sends, recvs

    to_half = table(128, 128, lambda s, d: jnp.where(s // 2 == d % 64, 0.25, 0.0))
    rim_map = table(128, 256, lambda s, d: (
        jnp.where((d < 16) & (s == 64 + d // 2), 1.0, 0.0)
        + jnp.where((d >= 240) & (s == 72 + d % 16 // 2), 1.0, 0.0)
        + jnp.where((d % 16 == 0) & (s == 80 + d // 32), 1.0, 0.0)
        + jnp.where((d % 16 == 15) & (s == 88 + d // 32), 1.0, 0.0)
    ))
    restrict_map = table(256, 128, lambda s, d: jnp.where(s // 32 * 8 + s % 16 // 2 == d, 0.25, 0.0))

    def packed_coarse(values):
        halves = apply_table(pair_rows(values), to_half)
        left = lax.broadcasted_iota(jnp.int32, (4, 8, 128), 2) < 64
        return jnp.where(left, halves[:4], halves[4:])

    coarse_k[1, a, 0] = packed_coarse(own[0])
    coarse_k[1, a, 1] = packed_coarse(own[1])

    pcond = pcond_ref[...]
    plane = lax.broadcasted_iota(jnp.int32, pcond.shape, 2)
    player = lax.broadcasted_iota(jnp.int32, pcond.shape, 1)
    p_east = jnp.where(plane < 240, 32.0 * (pcond + lanes(pcond, -16)), 0.0)
    p_north = jnp.where(plane % 16 < 15, 32.0 * (pcond + lanes(pcond, -1)), 0.0)
    p_above = jnp.where(player < 7, 0.5 * (pcond + layers(pcond, -1)), 0.0)
    outside = (
        jnp.where((plane < 16) | (plane >= 240), 64.0, 0.0)
        + jnp.where((plane % 16 == 0) | (plane % 16 == 15), 64.0, 0.0)
    )
    p_diag = (
        pcap_ref[...] + outside * pcond + p_east + lanes(p_east, 16)
        + p_north + lanes(p_north, 1) + p_above + layers(p_above, 1)
    )
    p_gain = RELAX / p_diag

    def p_around(values):
        return (
            p_east * lanes(values, -16) + lanes(p_east * values, 16)
            + p_north * lanes(values, -1) + lanes(p_north * values, 1)
            + p_above * layers(values, -1) + layers(p_above * values, 1)
        )

    wait_recv(halo_recv)
    count = 16 + 2 * HALO
    shape0 = (count, 8, 256)
    row0 = lax.broadcasted_iota(jnp.int32, shape0, 0)
    lane0 = lax.broadcasted_iota(jnp.int32, shape0, 2)
    left_i, right_i = has_left.astype(jnp.int32), has_right.astype(jnp.int32)
    up_i, down_i = has_up.astype(jnp.int32), has_down.astype(jnp.int32)
    inside0 = (
        (row0 >= HALO * (1 - up_i)) & (row0 < 16 + HALO + HALO * down_i)
        & ((lane0 < 128) | ((lane0 < 192) & (right_i > 0)) | ((lane0 >= 192) & (left_i > 0)))
    )
    last8 = lane % 16 < 8
    framed = []
    for index in range(3):
        body = jnp.concatenate([from_rows[0, index], own[index], from_rows[1, index]], axis=0)
        middle = [jnp.where(last8, from_side[0, p, index], from_side[1, p, index]) for p in range(2)]
        upper = jnp.where(last8, from_corner[0, 0, index], from_corner[0, 1, index])
        lower = jnp.where(last8, from_corner[1, 0, index], from_corner[1, 1, index])
        flank = []
        for x in range(-HALO, 16 + HALO):
            source = upper if x < 0 else lower if x >= 16 else middle[x // 8]
            flank.append(lanes(source, -(16 * (x % 8) + 8)))
        body = jnp.concatenate([body, jnp.stack(flank)], axis=2)
        framed.append(jnp.where(inside0, body, 0.0))
    stencil0 = stencil_of(framed[0], framed[1], 16.0, inside0)
    source0 = framed[2]
    u_a = smooth(stencil0[5] * source0, source0, stencil0)

    windows_into(u_a, slots)
    for r in range(32):
        out1[r] = slots[tables[r]]
    sends1, recvs1 = all_to_all(0, out1, in1)
    sends_k, recvs_k = gather(coarse_k, send_k, recv_k)
    r_0 = residual_of(u_a, source0, stencil0)[HALO:HALO + 16, :, :128]

    wait_recv(recvs1)
    for j in range(16):
        win1[j] = in1[froms[j]]
    first = win1[...]
    p_rhs = prhs_ref[...]
    p_edge = 64.0 * pcond
    p_source = p_rhs + p_edge * apply_table(first, rim_map)
    v_a = p_gain * p_source
    v_a = (1.0 - RELAX) * v_a + p_gain * (p_source + p_around(v_a))
    rest[...] = apply_table(p_source - p_diag * v_a + p_around(v_a), restrict_map)
    for r in range(32):
        out2[r] = rest[tables[64 + r]]
    sends2, recvs2 = all_to_all(1, out2, in2)

    wait_recv(recvs_k)
    rows1 = 8 * n_gx

    def spread_tiles(piece):
        left = lax.broadcasted_iota(jnp.int32, (4, 8, 128), 2) < 64
        blocks = []
        for t in range(n_gx):
            low, mid, high = piece(0, t), piece(1, t), piece(2, t)
            low_r, mid_r, high_r = lanes(low, 64), lanes(mid, 64), lanes(high, 64)
            blocks.append(jnp.concatenate([jnp.where(left, mid, high_r), low_r], axis=2))
            blocks.append(jnp.concatenate([jnp.where(left, mid_r, high), low], axis=2))
        return jnp.concatenate(blocks, axis=0)

    def inside_of(rows, width):
        lane_in = lax.broadcasted_iota(jnp.int32, (rows, 8, max(width * 4, 128)), 2)
        part = lane_in // width % 4
        return (part == 0) | ((part == 1) & (right_i > 0)) | ((part == 3) & (left_i > 0))

    halve_1 = table(256, 128, lambda s, d: jnp.where(s // 2 == d, 0.25, 0.0))
    halve_2 = to_half
    widen_3 = table(128, 128, lambda s, d: jnp.where(s == d // 2, 1.0, 0.0))
    widen_2 = table(128, 256, lambda s, d: jnp.where(s == d // 2, 1.0, 0.0))
    widen_1 = table(256, 256, lambda s, d: jnp.where(
        s == d // 2 + jnp.where(d >= 192, 128, 0), 1.0, 0.0))

    inside1 = inside_of(rows1, 64)
    k1 = jnp.where(inside1, spread_tiles(lambda s, t: coarse_k[s, t, 0]), 0.0)
    c1 = jnp.where(inside1, spread_tiles(lambda s, t: coarse_k[s, t, 1]), 0.0)
    k2, c2 = apply_table(pair_rows(k1), halve_1), apply_table(pair_rows(c1), halve_1)
    k3, c3 = apply_table(pair_rows(k2), halve_2), apply_table(pair_rows(c2), halve_2)
    stencil1 = stencil_of(k1, c1, 4.0, inside1)
    stencil2 = stencil_of(k2, c2, 1.0, inside_of(rows1 // 2, 32))
    stencil3 = stencil_of(k3, c3, 0.25, inside_of(rows1 // 4, 16))

    wait_recv(recvs2)
    pieces = []
    for band in range(2):
        items = []
        for col in range(16):
            at = tables[32 + 16 * band + col]
            flag = jnp.where(at >= 0, 1.0, 0.0).astype(F32)
            items.append(jnp.where(lane // 8 == 8, flag, in2[jnp.maximum(at, 0)]))
        placed = exchange_groups(items)
        for i in range(8):
            pieces.append(jnp.where(placed[8] > 0.5, placed[i], r_0[8 * band + i]))
    coarse_g[1, a] = packed_coarse(jnp.stack(pieces))
    sends_g, recvs_g = gather(coarse_g, send_g, recv_g)
    wait_recv(recvs_g)

    g1 = jnp.where(inside1, spread_tiles(lambda s, t: coarse_g[s, t]), 0.0)
    e1 = smooth(stencil1[5] * g1, g1, stencil1)
    g2 = apply_table(pair_rows(residual_of(e1, g1, stencil1)), halve_1)
    e2 = smooth(stencil2[5] * g2, g2, stencil2)
    g3 = apply_table(pair_rows(residual_of(e2, g2, stencil2)), halve_2)
    e3 = stencil3[5] * g3
    e3 = lax.fori_loop(0, SWEEPS - 1, lambda _, v: smooth(v, g3, stencil3), e3)
    e2 = smooth(e2 + apply_table(repeat_rows(e3), widen_3), g2, stencil2)
    e1 = smooth(e1 + apply_table(repeat_rows(e2), widen_2), g1, stencil1)
    column[pl.ds(0, 2)] = jnp.zeros((2, 8, 256), F32)
    column[pl.ds(rows1 + 2, 2)] = jnp.zeros((2, 8, 256), F32)
    column[pl.ds(2, rows1)] = e1
    near = column[pl.ds(8 * a, 12)]
    u_b = u_a + jnp.where(inside0, apply_table(repeat_rows(near), widen_1), 0.0)
    solved = smooth(u_b, source0, stencil0)

    windows_into(solved, slots)
    for r in range(32):
        out3[r] = slots[tables[r]]
    sends3, recvs3 = all_to_all(2, out3, in3)
    for x in range(16):
        field_ref[pl.ds(x, 8, stride=16), :] = solved[HALO + x, :, :128]
    grow_map = table(128, 256, lambda s, d: jnp.where(s == d // 32 * 8 + d % 16 // 2, 1.0, 0.0))
    wait_recv(recvs3)
    for j in range(16):
        win2[j] = in3[froms[j]]
    second = win2[...]
    values = v_a + apply_table(second - first, grow_map)
    p_source = p_rhs + p_edge * apply_table(second, rim_map)
    patch_ref[...] = (1.0 - RELAX) * values + p_gain * (p_source + p_around(values))

    for copies in (halo_send, sends1, sends_k, sends2, sends_g, sends3):
        wait_send(copies)


def body(n_gx, n_gy, rhs_base, cond_base, cap_base, patch_rhs, patch_cond, patch_cap, box_list, patch_from):
    rows_all = 2 * patch_rhs.shape[0]
    cap_rows = rows_all // n_gy
    ids = lax.broadcasted_iota(jnp.int32, (rows_all, 1), 0)
    slot_ids, send_rows = box_list[:, 0][None, :], box_list[:, 1][None, :]
    owned = lax.broadcasted_iota(jnp.int32, (1, patch_from.shape[0]), 1)
    tables = jnp.concatenate([
        jnp.max(jnp.where(send_rows == ids, slot_ids, 0), axis=1),
        jnp.max(jnp.where(slot_ids == ids, send_rows, -1), axis=1),
        jnp.max(jnp.where(patch_from[None, :] == ids, owned, 0), axis=1),
    ])
    vmem = pl.BlockSpec(memory_space=pltpu.VMEM)
    smem = pl.BlockSpec(memory_space=pltpu.SMEM)
    dma = pltpu.SemaphoreType.DMA
    buffer = pltpu.VMEM((32, 8, 128), F32)
    field, patches = pl.pallas_call(
        functools.partial(kernel, n_gx, n_gy, cap_rows),
        out_shape=(
            jax.ShapeDtypeStruct((128, 128), F32),
            jax.ShapeDtypeStruct(patch_rhs.shape, F32),
        ),
        in_specs=[smem, smem] + [vmem] * 6,
        out_specs=(vmem, vmem),
        scratch_shapes=[
            pltpu.VMEM((3, 16, 8, 128), F32),
            pltpu.VMEM((2, 3, 8, 128), F32),
            pltpu.VMEM((2, 3, HALO, 8, 128), F32),
            pltpu.VMEM((2, 2, 3, 8, 128), F32),
            pltpu.VMEM((2, 2, 3, 8, 128), F32),
            buffer, buffer, buffer, buffer, buffer, buffer, buffer,
            pltpu.VMEM((16, 8, 128), F32),
            pltpu.VMEM((16, 8, 128), F32),
            pltpu.VMEM((16, 8, 128), F32),
            pltpu.VMEM((3, n_gx, 2, 4, 8, 128), F32),
            pltpu.VMEM((3, n_gx, 4, 8, 128), F32),
            pltpu.VMEM((8 * n_gx + 4, 8, 256), F32),
            dma((9,)), dma((9,)),
            dma((3, n_gy)), dma((3, n_gy)),
            dma((3, n_gx)), dma((3, n_gx)),
            dma((3, n_gx)), dma((3, n_gx)),
        ],
        compiler_params=pltpu.CompilerParams(
            collective_id=0, has_side_effects=True, vmem_limit_bytes=48 * 1024 * 1024
        ),
    )(
        tables, patch_from,
        rhs_base.reshape(128, 128), cond_base.reshape(128, 128), cap_base.reshape(128, 128),
        patch_rhs, patch_cond, patch_cap,
    )
    return field.reshape(rhs_base.shape), patches


def solution(mesh):
    return jax.shard_map(
        functools.partial(body, mesh.shape["gx"], mesh.shape["gy"]),
        mesh=mesh,
        in_specs=(
            P(None, "gx", "gy"),
            P(None, "gx", "gy"),
            P(None, "gx", "gy"),
            P(("gx", "gy"), None, None),
            P(("gx", "gy"), None, None),
            P(("gx", "gy"), None, None),
            P(("gx", "gy"), None),
            P(("gx", "gy")),
        ),
        out_specs=(P(None, "gx", "gy"), P(("gx", "gy"), None, None)),
        check_vma=False,
    )
```

```python
import functools
import jax
import jax.numpy as jnp
from jax import lax
from jax.experimental import pallas as pl
from jax.experimental.pallas import tpu as pltpu
from jax.sharding import PartitionSpec as P

SWEEPS = 12
RELAX = 0.8
F32 = jnp.float32
HALO = 4
MESH = pl.DeviceIdType.MESH


def table(rows, cols, rule):
    src = lax.broadcasted_iota(jnp.int32, (rows, cols), 0)
    dst = lax.broadcasted_iota(jnp.int32, (rows, cols), 1)
    return rule(src, dst).astype(jnp.bfloat16)


def apply_table(values, matrix):
    lead = values.shape[:-1]
    flat = values.reshape(-1, values.shape[-1])
    high = flat.astype(jnp.bfloat16)
    low = (flat - high.astype(F32)).astype(jnp.bfloat16)
    out = jnp.dot(high, matrix, preferred_element_type=F32) + jnp.dot(
        low, matrix, preferred_element_type=F32
    )
    return out.reshape(lead + (matrix.shape[1],))


def lanes(values, shift):
    return pltpu.roll(values, shift % values.shape[-1], values.ndim - 1)


def layers(values, shift):
    return pltpu.roll(values, shift % 8, values.ndim - 2)


def rows_up(values):
    return jnp.concatenate([values[1:], jnp.zeros_like(values[:1])], axis=0)


def rows_down(values):
    return jnp.concatenate([jnp.zeros_like(values[:1]), values[:-1]], axis=0)


def stencil_of(conduct, capacity, weight, mask):
    half = 0.5 * weight
    layer = lax.broadcasted_iota(jnp.int32, conduct.shape, 1)
    east = half * (conduct + rows_up(conduct))
    west = half * (conduct + rows_down(conduct))
    north = half * (conduct + lanes(conduct, -1))
    above = jnp.where(layer < 7, 0.5 * (conduct + layers(conduct, -1)), 0.0)
    diagonal = (
        capacity + east + west + north + lanes(north, 1) + above + layers(above, 1)
    )
    gain = jnp.where(mask, RELAX / diagonal, 0.0)
    return (east, west, north, above, diagonal, gain)


def around(values, stencil):
    east, west, north, above, _, _ = stencil
    return (
        east * rows_up(values)
        + west * rows_down(values)
        + north * lanes(values, -1)
        + lanes(north * values, 1)
        + above * layers(values, -1)
        + layers(above * values, 1)
    )


def smooth(values, source, stencil):
    return (1.0 - RELAX) * values + stencil[5] * (source + around(values, stencil))


def residual_of(values, source, stencil):
    return source - stencil[4] * values + around(values, stencil)


def pair_rows(values):
    count = values.shape[0] // 2
    split = values.reshape((count, 2) + values.shape[1:])
    return split[:, 0] + split[:, 1]


def repeat_rows(values):
    count = values.shape[0]
    return jnp.broadcast_to(values[:, None], (count, 2) + values.shape[1:]).reshape(
        (2 * count,) + values.shape[1:]
    )


def exchange_groups(items):
    group = lax.broadcasted_iota(jnp.int32, (8, 128), 1) // 8
    turned = [items[(-n) % 16] for n in range(16)]
    turned = [lanes(v, 8 * ((-n) % 16)) if n else v for n, v in enumerate(turned)]
    for bit in range(4):
        step = 1 << bit
        picked = (group // step) % 2 == 1
        turned = [jnp.where(picked, turned[(n - step) % 16], turned[n]) for n in range(16)]
    return [lanes(v, -8 * n) if n else v for n, v in enumerate(turned)]


def windows_into(field, out_ref):
    lane = lax.broadcasted_iota(jnp.int32, (8, 128), 1)
    for band in range(2):
        first = HALO + 8 * band
        items = [field[first + i, :, :128] for i in range(8)]
        south = jnp.zeros((8, 128), F32)
        north = jnp.zeros((8, 128), F32)
        for i in range(8):
            edge = jnp.where((lane == 0) | (lane == 127), field[first + i, :, 128:], items[i])
            south = jnp.where(lane % 8 == i, lanes(edge, i + 1), south)
            north = jnp.where(lane % 8 == i, lanes(edge, i - 8), north)
        items = items + [field[first - 1, :, :128], field[first + 8, :, :128], south, north]
        items = items + [jnp.zeros((8, 128), F32)] * 4
        for col, window in enumerate(exchange_groups(items)):
            out_ref[16 * band + col] = window


def kernel(
    n_gx, n_gy, cap_rows, boxes_hbm, froms_hbm,
    rhs_hbm, cond_hbm, capb_hbm, prhs_hbm, pcond_hbm, pcap_hbm,
    field_ref, patch_ref,
    boxes, froms, lists, routes, cond_ref, capb_ref, rhs_ref, pcond_ref, pcap_ref, prhs_ref,
    load_sem, tile, side, from_rows, from_side, from_corner,
    slots, out1, in1, out2, in2, out3, in3, win1, win2, rest,
    coarse_k, coarse_g, column,
    send_a, recv_a, send_x, recv_x, send_k, recv_k, send_g, recv_g,
):
    a = lax.axis_index("gx")
    b = lax.axis_index("gy")
    has_up, has_down = a > 0, a < n_gx - 1
    has_left, has_right = b > 0, b < n_gy - 1
    ok_gx = {-1: has_up, 0: None, 1: has_down}
    ok_gy = {-1: has_left, 0: None, 1: has_right}

    def guarded(cond, action):
        if cond is None:
            action()
        else:
            pl.when(cond)(action)

    loads = [
        pltpu.make_async_copy(src, dst, load_sem.at[i])
        for i, (src, dst) in enumerate((
            (cond_hbm, cond_ref), (capb_hbm, capb_ref), (rhs_hbm, rhs_ref), (boxes_hbm, boxes),
            (froms_hbm, froms), (pcond_hbm, pcond_ref), (pcap_hbm, pcap_ref), (prhs_hbm, prhs_ref),
        ))
    ]
    for load in loads:
        load.start()

    barrier = pltpu.get_barrier_semaphore()

    def greet(x, y):
        pl.semaphore_signal(barrier, inc=1, device_id=(x, y), device_id_type=MESH)

    for d in range(1, n_gy):
        greet(a, lax.rem(b + d, n_gy))
    for d in range(1, n_gx):
        for dy in (-1, 0, 1):
            guarded(ok_gy[dy], lambda d=d, dy=dy: greet(lax.rem(a + d, n_gx), b + dy))
    columns = 1 + has_left.astype(jnp.int32) + has_right.astype(jnp.int32)

    lane = lax.broadcasted_iota(jnp.int32, (8, 128), 1)
    own = []
    for index, ref in enumerate((cond_ref, capb_ref, rhs_ref)):
        loads[index].wait()
        rows = [ref[pl.ds(x, 8, stride=16), :] for x in range(16)]
        for x in range(16):
            tile[index, x] = rows[x]
        for part in range(2):
            packed = lanes(rows[8 * part], 8)
            for i in range(1, 8):
                packed = jnp.where(lane // 16 == i, lanes(rows[8 * part + i], 8 + 16 * i), packed)
            side[part, index] = packed
        own.append(jnp.stack(rows))

    pl.semaphore_wait(barrier, n_gy - 1 + (n_gx - 1) * columns)

    def start_wait(copies):
        for cond, make in copies:
            guarded(cond, lambda make=make: make().start())

    def wait_recv(copies):
        for cond, make in copies:
            guarded(cond, lambda make=make: make().wait_recv())

    def wait_send(copies):
        for cond, make in copies:
            guarded(cond, lambda make=make: make().wait_send())

    def remote(src, dst, ssem, rsem, x, y):
        return pltpu.make_async_remote_copy(
            src_ref=src, dst_ref=dst, send_sem=ssem, recv_sem=rsem,
            device_id=(x, y), device_id_type=MESH,
        )

    halo_send, halo_recv = [], []
    for dx in (-1, 0, 1):
        for dy in (-1, 0, 1):
            if dx == 0 and dy == 0:
                continue
            conds = [c for c in (ok_gx[dx], ok_gy[dy]) if c is not None]
            cond = conds[0] if len(conds) == 1 else jnp.logical_and(conds[0], conds[1])
            place = 3 * (dx + 1) + dy + 1
            back = 3 * (1 - dx) + 1 - dy

            def views(dx=dx, dy=dy):
                if dy == 0:
                    start = 0 if dx < 0 else 16 - HALO
                    return tile.at[:, pl.ds(start, HALO)], from_rows.at[(1 - dx) // 2]
                if dx == 0:
                    return side, from_side.at[(1 - dy) // 2]
                part = 0 if dx < 0 else 1
                return side.at[part], from_corner.at[(1 - dx) // 2, (1 - dy) // 2]

            def landing(dx=dx, dy=dy):
                if dy == 0:
                    return from_rows.at[(1 + dx) // 2]
                if dx == 0:
                    return from_side.at[(1 + dy) // 2]
                return from_corner.at[(1 + dx) // 2, (1 + dy) // 2]

            def out(views=views, dx=dx, dy=dy, place=place, back=back):
                src, dst = views()
                return remote(src, dst, send_a.at[place], recv_a.at[back], a + dx, b + dy)

            def arrive(landing=landing, dx=dx, dy=dy, place=place):
                return remote(landing(), landing(), send_a.at[place], recv_a.at[place], a + dx, b + dy)

            halo_send.append((cond, out))
            halo_recv.append((cond, arrive))
    start_wait(halo_send)

    def all_to_all(phase, src, dst):
        sends, recvs = [], []
        for d in range(1, n_gy):
            def out(d=d):
                to = lax.rem(b + d, n_gy)
                return remote(
                    src.at[pl.ds(to * cap_rows, cap_rows)], dst.at[pl.ds(b * cap_rows, cap_rows)],
                    send_x.at[phase, d], recv_x.at[phase, d], a, to,
                )

            def arrive(d=d):
                at = lax.rem(b + n_gy - d, n_gy)
                piece = dst.at[pl.ds(at * cap_rows, cap_rows)]
                return remote(piece, piece, send_x.at[phase, d], recv_x.at[phase, d], a, at)

            sends.append((None, out))
            recvs.append((None, arrive))
        start_wait(sends)
        mine = pl.ds(b * cap_rows, cap_rows)
        dst[mine] = src[mine]
        return sends, recvs

    def gather(buffer, ssem, rsem):
        sends, recvs = [], []
        for dy in (0, -1, 1):
            for d in range(n_gx):
                if dy == 0 and d == 0:
                    continue

                def out(d=d, dy=dy):
                    to = lax.rem(a + d, n_gx)
                    return remote(
                        buffer.at[1, a], buffer.at[1 - dy, a],
                        ssem.at[dy + 1, d], rsem.at[1 - dy, d], to, b + dy,
                    )

                def arrive(d=d, dy=dy):
                    at = lax.rem(a + n_gx - d, n_gx)
                    piece = buffer.at[dy + 1, at]
                    return remote(piece, piece, ssem.at[dy + 1, d], rsem.at[dy + 1, d], at, b + dy)

                sends.append((ok_gy[dy], out))
                recvs.append((ok_gy[dy], arrive))
        start_wait(sends)
        return sends, recvs

    loads[3].wait()
    loads[4].wait()
    list_lane = lax.broadcasted_iota(jnp.int32, (1, 128), 1)
    by_row = jnp.zeros((1, 128), jnp.int32)
    by_slot = jnp.full((1, 128), -1, jnp.int32)
    by_from = jnp.zeros((1, 128), jnp.int32)
    for k in range(32):
        slot, row = boxes[0, k], boxes[1, k]
        by_row = jnp.where(list_lane == row, slot, by_row)
        by_slot = jnp.where(list_lane == slot, row, by_slot)
    for j in range(16):
        by_from = jnp.where(list_lane == froms[j], j, by_from)
    lists[0:1] = by_row
    lists[1:2] = by_slot
    lists[2:3] = by_from
    lists[3:8] = jnp.zeros((5, 128), jnp.int32)
    route = pltpu.make_async_copy(lists, routes, load_sem.at[8])
    route.start()

    to_half = table(128, 128, lambda s, d: jnp.where(s // 2 == d % 64, 0.25, 0.0))
    rim_map = table(128, 256, lambda s, d: (
        jnp.where((d < 16) & (s == 64 + d // 2), 1.0, 0.0)
        + jnp.where((d >= 240) & (s == 72 + d % 16 // 2), 1.0, 0.0)
        + jnp.where((d % 16 == 0) & (s == 80 + d // 32), 1.0, 0.0)
        + jnp.where((d % 16 == 15) & (s == 88 + d // 32), 1.0, 0.0)
    ))
    restrict_map = table(256, 128, lambda s, d: jnp.where(s // 32 * 8 + s % 16 // 2 == d, 0.25, 0.0))

    def packed_coarse(values):
        halves = apply_table(pair_rows(values), to_half)
        left = lax.broadcasted_iota(jnp.int32, (4, 8, 128), 2) < 64
        return jnp.where(left, halves[:4], halves[4:])

    coarse_k[1, a, 0] = packed_coarse(own[0])
    coarse_k[1, a, 1] = packed_coarse(own[1])

    for load in loads[5:]:
        load.wait()
    pcond = pcond_ref[...]
    plane = lax.broadcasted_iota(jnp.int32, pcond.shape, 2)
    player = lax.broadcasted_iota(jnp.int32, pcond.shape, 1)
    p_east = jnp.where(plane < 240, 32.0 * (pcond + lanes(pcond, -16)), 0.0)
    p_north = jnp.where(plane % 16 < 15, 32.0 * (pcond + lanes(pcond, -1)), 0.0)
    p_above = jnp.where(player < 7, 0.5 * (pcond + layers(pcond, -1)), 0.0)
    outside = (
        jnp.where((plane < 16) | (plane >= 240), 64.0, 0.0)
        + jnp.where((plane % 16 == 0) | (plane % 16 == 15), 64.0, 0.0)
    )
    p_diag = (
        pcap_ref[...] + outside * pcond + p_east + lanes(p_east, 16)
        + p_north + lanes(p_north, 1) + p_above + layers(p_above, 1)
    )
    p_gain = RELAX / p_diag

    def p_around(values):
        return (
            p_east * lanes(values, -16) + lanes(p_east * values, 16)
            + p_north * lanes(values, -1) + lanes(p_north * values, 1)
            + p_above * layers(values, -1) + layers(p_above * values, 1)
        )

    route.wait()

    wait_recv(halo_recv)
    count = 16 + 2 * HALO
    shape0 = (count, 8, 256)
    row0 = lax.broadcasted_iota(jnp.int32, shape0, 0)
    lane0 = lax.broadcasted_iota(jnp.int32, shape0, 2)
    left_i, right_i = has_left.astype(jnp.int32), has_right.astype(jnp.int32)
    up_i, down_i = has_up.astype(jnp.int32), has_down.astype(jnp.int32)
    inside0 = (
        (row0 >= HALO * (1 - up_i)) & (row0 < 16 + HALO + HALO * down_i)
        & ((lane0 < 128) | ((lane0 < 192) & (right_i > 0)) | ((lane0 >= 192) & (left_i > 0)))
    )
    last8 = lane % 16 < 8
    framed = []
    for index in range(3):
        body = jnp.concatenate([from_rows[0, index], own[index], from_rows[1, index]], axis=0)
        middle = [jnp.where(last8, from_side[0, p, index], from_side[1, p, index]) for p in range(2)]
        upper = jnp.where(last8, from_corner[0, 0, index], from_corner[0, 1, index])
        lower = jnp.where(last8, from_corner[1, 0, index], from_corner[1, 1, index])
        flank = []
        for x in range(-HALO, 16 + HALO):
            source = upper if x < 0 else lower if x >= 16 else middle[x // 8]
            flank.append(lanes(source, -(16 * (x % 8) + 8)))
        body = jnp.concatenate([body, jnp.stack(flank)], axis=2)
        framed.append(jnp.where(inside0, body, 0.0))
    stencil0 = stencil_of(framed[0], framed[1], 16.0, inside0)
    source0 = framed[2]
    u_a = smooth(stencil0[5] * source0, source0, stencil0)

    windows_into(u_a, slots)
    for r in range(32):
        out1[r] = slots[routes[0, r]]
    sends1, recvs1 = all_to_all(0, out1, in1)
    sends_k, recvs_k = gather(coarse_k, send_k, recv_k)
    r_0 = residual_of(u_a, source0, stencil0)[HALO:HALO + 16, :, :128]

    wait_recv(recvs1)
    for j in range(16):
        win1[j] = in1[froms[j]]
    first = win1[...]
    p_rhs = prhs_ref[...]
    p_edge = 64.0 * pcond
    p_source = p_rhs + p_edge * apply_table(first, rim_map)
    v_a = p_gain * p_source
    v_a = (1.0 - RELAX) * v_a + p_gain * (p_source + p_around(v_a))
    rest[...] = apply_table(p_source - p_diag * v_a + p_around(v_a), restrict_map)
    for r in range(32):
        out2[r] = rest[routes[2, r]]
    sends2, recvs2 = all_to_all(1, out2, in2)

    wait_recv(recvs_k)
    rows1 = 8 * n_gx

    def spread_tiles(piece):
        left = lax.broadcasted_iota(jnp.int32, (4, 8, 128), 2) < 64
        blocks = []
        for t in range(n_gx):
            low, mid, high = piece(0, t), piece(1, t), piece(2, t)
            low_r, mid_r, high_r = lanes(low, 64), lanes(mid, 64), lanes(high, 64)
            blocks.append(jnp.concatenate([jnp.where(left, mid, high_r), low_r], axis=2))
            blocks.append(jnp.concatenate([jnp.where(left, mid_r, high), low], axis=2))
        return jnp.concatenate(blocks, axis=0)

    def inside_of(rows, width):
        lane_in = lax.broadcasted_iota(jnp.int32, (rows, 8, max(width * 4, 128)), 2)
        part = lane_in // width % 4
        return (part == 0) | ((part == 1) & (right_i > 0)) | ((part == 3) & (left_i > 0))

    halve_1 = table(256, 128, lambda s, d: jnp.where(s // 2 == d, 0.25, 0.0))
    halve_2 = to_half
    widen_3 = table(128, 128, lambda s, d: jnp.where(s == d // 2, 1.0, 0.0))
    widen_2 = table(128, 256, lambda s, d: jnp.where(s == d // 2, 1.0, 0.0))
    widen_1 = table(256, 256, lambda s, d: jnp.where(
        s == d // 2 + jnp.where(d >= 192, 128, 0), 1.0, 0.0))

    inside1 = inside_of(rows1, 64)
    k1 = jnp.where(inside1, spread_tiles(lambda s, t: coarse_k[s, t, 0]), 0.0)
    c1 = jnp.where(inside1, spread_tiles(lambda s, t: coarse_k[s, t, 1]), 0.0)
    k2, c2 = apply_table(pair_rows(k1), halve_1), apply_table(pair_rows(c1), halve_1)
    k3, c3 = apply_table(pair_rows(k2), halve_2), apply_table(pair_rows(c2), halve_2)
    stencil1 = stencil_of(k1, c1, 4.0, inside1)
    stencil2 = stencil_of(k2, c2, 1.0, inside_of(rows1 // 2, 32))
    stencil3 = stencil_of(k3, c3, 0.25, inside_of(rows1 // 4, 16))

    wait_recv(recvs2)
    pieces = []
    for band in range(2):
        items = []
        for col in range(16):
            at = routes[1, 16 * band + col]
            flag = jnp.where(at >= 0, 1.0, 0.0).astype(F32)
            items.append(jnp.where(lane // 8 == 8, flag, in2[jnp.maximum(at, 0)]))
        placed = exchange_groups(items)
        for i in range(8):
            pieces.append(jnp.where(placed[8] > 0.5, placed[i], r_0[8 * band + i]))
    coarse_g[1, a] = packed_coarse(jnp.stack(pieces))
    sends_g, recvs_g = gather(coarse_g, send_g, recv_g)
    wait_recv(recvs_g)

    g1 = jnp.where(inside1, spread_tiles(lambda s, t: coarse_g[s, t]), 0.0)
    e1 = smooth(stencil1[5] * g1, g1, stencil1)
    g2 = apply_table(pair_rows(residual_of(e1, g1, stencil1)), halve_1)
    e2 = smooth(stencil2[5] * g2, g2, stencil2)
    g3 = apply_table(pair_rows(residual_of(e2, g2, stencil2)), halve_2)
    e3 = stencil3[5] * g3
    e3 = lax.fori_loop(0, SWEEPS - 1, lambda _, v: smooth(v, g3, stencil3), e3)
    e2 = smooth(e2 + apply_table(repeat_rows(e3), widen_3), g2, stencil2)
    e1 = smooth(e1 + apply_table(repeat_rows(e2), widen_2), g1, stencil1)
    column[pl.ds(0, 2)] = jnp.zeros((2, 8, 256), F32)
    column[pl.ds(rows1 + 2, 2)] = jnp.zeros((2, 8, 256), F32)
    column[pl.ds(2, rows1)] = e1
    near = column[pl.ds(8 * a, 12)]
    u_b = u_a + jnp.where(inside0, apply_table(repeat_rows(near), widen_1), 0.0)
    solved = smooth(u_b, source0, stencil0)

    windows_into(solved, slots)
    for r in range(32):
        out3[r] = slots[routes[0, r]]
    sends3, recvs3 = all_to_all(2, out3, in3)
    for x in range(16):
        field_ref[pl.ds(x, 8, stride=16), :] = solved[HALO + x, :, :128]
    grow_map = table(128, 256, lambda s, d: jnp.where(s == d // 32 * 8 + d % 16 // 2, 1.0, 0.0))
    wait_recv(recvs3)
    for j in range(16):
        win2[j] = in3[froms[j]]
    second = win2[...]
    values = v_a + apply_table(second - first, grow_map)
    p_source = p_rhs + p_edge * apply_table(second, rim_map)
    patch_ref[...] = (1.0 - RELAX) * values + p_gain * (p_source + p_around(values))

    for copies in (halo_send, sends1, sends_k, sends2, sends_g, sends3):
        wait_send(copies)


def body(n_gx, n_gy, rhs_base, cond_base, cap_base, patch_rhs, patch_cond, patch_cap, box_list, patch_from):
    cap_rows = 2 * patch_rhs.shape[0] // n_gy
    vmem = pl.BlockSpec(memory_space=pltpu.VMEM)
    far = pl.BlockSpec(memory_space=pltpu.HBM)
    dma = pltpu.SemaphoreType.DMA
    buffer = pltpu.VMEM((32, 8, 128), F32)
    field, patches = pl.pallas_call(
        functools.partial(kernel, n_gx, n_gy, cap_rows),
        out_shape=(
            jax.ShapeDtypeStruct((128, 128), F32),
            jax.ShapeDtypeStruct(patch_rhs.shape, F32),
        ),
        in_specs=[far] * 8,
        out_specs=(vmem, vmem),
        scratch_shapes=[
            pltpu.SMEM((2, 32), jnp.int32), pltpu.SMEM((16,), jnp.int32),
            pltpu.VMEM((8, 128), jnp.int32), pltpu.SMEM((8, 128), jnp.int32),
            pltpu.VMEM((128, 128), F32), pltpu.VMEM((128, 128), F32), pltpu.VMEM((128, 128), F32),
            pltpu.VMEM(patch_rhs.shape, F32), pltpu.VMEM(patch_rhs.shape, F32),
            pltpu.VMEM(patch_rhs.shape, F32), dma((9,)),
            pltpu.VMEM((3, 16, 8, 128), F32),
            pltpu.VMEM((2, 3, 8, 128), F32),
            pltpu.VMEM((2, 3, HALO, 8, 128), F32),
            pltpu.VMEM((2, 2, 3, 8, 128), F32),
            pltpu.VMEM((2, 2, 3, 8, 128), F32),
            buffer, buffer, buffer, buffer, buffer, buffer, buffer,
            pltpu.VMEM((16, 8, 128), F32),
            pltpu.VMEM((16, 8, 128), F32),
            pltpu.VMEM((16, 8, 128), F32),
            pltpu.VMEM((3, n_gx, 2, 4, 8, 128), F32),
            pltpu.VMEM((3, n_gx, 4, 8, 128), F32),
            pltpu.VMEM((8 * n_gx + 4, 8, 256), F32),
            dma((9,)), dma((9,)),
            dma((3, n_gy)), dma((3, n_gy)),
            dma((3, n_gx)), dma((3, n_gx)),
            dma((3, n_gx)), dma((3, n_gx)),
        ],
        compiler_params=pltpu.CompilerParams(
            collective_id=0, has_side_effects=True, vmem_limit_bytes=64 * 1024 * 1024
        ),
    )(
        box_list.T, patch_from,
        rhs_base.reshape(128, 128), cond_base.reshape(128, 128), cap_base.reshape(128, 128),
        patch_rhs, patch_cond, patch_cap,
    )
    return field.reshape(rhs_base.shape), patches


def solution(mesh):
    return jax.shard_map(
        functools.partial(body, mesh.shape["gx"], mesh.shape["gy"]),
        mesh=mesh,
        in_specs=(
            P(None, "gx", "gy"),
            P(None, "gx", "gy"),
            P(None, "gx", "gy"),
            P(("gx", "gy"), None, None),
            P(("gx", "gy"), None, None),
            P(("gx", "gy"), None, None),
            P(("gx", "gy"), None),
            P(("gx", "gy")),
        ),
        out_specs=(P(None, "gx", "gy"), P(("gx", "gy"), None, None)),
        check_vma=False,
    )
```

```python
import functools
import jax
import jax.numpy as jnp
from jax import lax
from jax.experimental import pallas as pl
from jax.experimental.pallas import tpu as pltpu
from jax.sharding import PartitionSpec as P

SWEEPS = 12
RELAX = 0.8
F32 = jnp.float32
HALO = 4
MESH = pl.DeviceIdType.MESH


def table(rows, cols, rule):
    src = lax.broadcasted_iota(jnp.int32, (rows, cols), 0)
    dst = lax.broadcasted_iota(jnp.int32, (rows, cols), 1)
    return rule(src, dst).astype(jnp.bfloat16)


def apply_table(values, matrix):
    lead = values.shape[:-1]
    flat = values.reshape(-1, values.shape[-1])
    high = flat.astype(jnp.bfloat16)
    low = (flat - high.astype(F32)).astype(jnp.bfloat16)
    out = jnp.dot(high, matrix, preferred_element_type=F32) + jnp.dot(
        low, matrix, preferred_element_type=F32
    )
    return out.reshape(lead + (matrix.shape[1],))


def lanes(values, shift):
    return pltpu.roll(values, shift % values.shape[-1], values.ndim - 1)


def layers(values, shift):
    return pltpu.roll(values, shift % 8, values.ndim - 2)


def rows_up(values):
    return jnp.concatenate([values[1:], jnp.zeros_like(values[:1])], axis=0)


def rows_down(values):
    return jnp.concatenate([jnp.zeros_like(values[:1]), values[:-1]], axis=0)


def stencil_of(conduct, capacity, weight, mask):
    half = 0.5 * weight
    layer = lax.broadcasted_iota(jnp.int32, conduct.shape, 1)
    east = half * (conduct + rows_up(conduct))
    west = half * (conduct + rows_down(conduct))
    north = half * (conduct + lanes(conduct, -1))
    above = jnp.where(layer < 7, 0.5 * (conduct + layers(conduct, -1)), 0.0)
    diagonal = (
        capacity + east + west + north + lanes(north, 1) + above + layers(above, 1)
    )
    gain = jnp.where(mask, RELAX / diagonal, 0.0)
    return (east, west, north, above, diagonal, gain)


def around(values, stencil):
    east, west, north, above, _, _ = stencil
    return (
        east * rows_up(values)
        + west * rows_down(values)
        + north * lanes(values, -1)
        + lanes(north * values, 1)
        + above * layers(values, -1)
        + layers(above * values, 1)
    )


def smooth(values, source, stencil):
    return (1.0 - RELAX) * values + stencil[5] * (source + around(values, stencil))


def residual_of(values, source, stencil):
    return source - stencil[4] * values + around(values, stencil)


def pair_rows(values):
    count = values.shape[0] // 2
    split = values.reshape((count, 2) + values.shape[1:])
    return split[:, 0] + split[:, 1]


def repeat_rows(values):
    count = values.shape[0]
    return jnp.broadcast_to(values[:, None], (count, 2) + values.shape[1:]).reshape(
        (2 * count,) + values.shape[1:]
    )


def exchange_groups(items):
    group = lax.broadcasted_iota(jnp.int32, (8, 128), 1) // 8
    turned = [items[(-n) % 16] for n in range(16)]
    turned = [lanes(v, 8 * ((-n) % 16)) if n else v for n, v in enumerate(turned)]
    for bit in range(4):
        step = 1 << bit
        picked = (group // step) % 2 == 1
        turned = [jnp.where(picked, turned[(n - step) % 16], turned[n]) for n in range(16)]
    return [lanes(v, -8 * n) if n else v for n, v in enumerate(turned)]


def windows_into(field, out_ref):
    lane = lax.broadcasted_iota(jnp.int32, (8, 128), 1)
    for band in range(2):
        first = HALO + 8 * band
        items = [field[first + i, :, :128] for i in range(8)]
        south = jnp.zeros((8, 128), F32)
        north = jnp.zeros((8, 128), F32)
        for i in range(8):
            edge = jnp.where((lane == 0) | (lane == 127), field[first + i, :, 128:], items[i])
            south = jnp.where(lane % 8 == i, lanes(edge, i + 1), south)
            north = jnp.where(lane % 8 == i, lanes(edge, i - 8), north)
        items = items + [field[first - 1, :, :128], field[first + 8, :, :128], south, north]
        items = items + [jnp.zeros((8, 128), F32)] * 4
        for col, window in enumerate(exchange_groups(items)):
            out_ref[16 * band + col] = window


def kernel(
    n_gx, n_gy, cap_rows, boxes_hbm, froms_hbm,
    rhs_hbm, cond_hbm, capb_hbm, prhs_hbm, pcond_hbm, pcap_hbm,
    field_ref, patch_ref,
    boxes, froms, lists, routes, cond_ref, capb_ref, rhs_ref, pcond_ref, pcap_ref, prhs_ref,
    load_sem, tile, side, from_rows, from_side, from_corner,
    slots, out1, in1, out2, in2, out3, in3, win1, win2, rest,
    coarse_k, coarse_g, column,
    send_a, recv_a, send_x, recv_x, send_k, recv_k, send_g, recv_g,
):
    a = lax.axis_index("gx")
    b = lax.axis_index("gy")
    has_up, has_down = a > 0, a < n_gx - 1
    has_left, has_right = b > 0, b < n_gy - 1
    ok_gx = {-1: has_up, 0: None, 1: has_down}
    ok_gy = {-1: has_left, 0: None, 1: has_right}

    def guarded(cond, action):
        if cond is None:
            action()
        else:
            pl.when(cond)(action)

    loads = [
        pltpu.make_async_copy(src, dst, load_sem.at[i])
        for i, (src, dst) in enumerate((
            (cond_hbm, cond_ref), (capb_hbm, capb_ref), (rhs_hbm, rhs_ref), (boxes_hbm, boxes),
            (froms_hbm, froms), (pcond_hbm, pcond_ref), (pcap_hbm, pcap_ref), (prhs_hbm, prhs_ref),
        ))
    ]
    for load in loads:
        load.start()

    barrier = pltpu.get_barrier_semaphore()

    def greet(x, y):
        pl.semaphore_signal(barrier, inc=1, device_id=(x, y), device_id_type=MESH)

    for d in range(1, n_gy):
        greet(a, lax.rem(b + d, n_gy))
    for d in range(1, n_gx):
        for dy in (-1, 0, 1):
            guarded(ok_gy[dy], lambda d=d, dy=dy: greet(lax.rem(a + d, n_gx), b + dy))
    columns = 1 + has_left.astype(jnp.int32) + has_right.astype(jnp.int32)

    lane = lax.broadcasted_iota(jnp.int32, (8, 128), 1)
    own = []
    for index, ref in enumerate((cond_ref, capb_ref, rhs_ref)):
        loads[index].wait()
        rows = [ref[pl.ds(x, 8, stride=16), :] for x in range(16)]
        for x in range(16):
            tile[index, x] = rows[x]
        for part in range(2):
            packed = lanes(rows[8 * part], 8)
            for i in range(1, 8):
                packed = jnp.where(lane // 16 == i, lanes(rows[8 * part + i], 8 + 16 * i), packed)
            side[part, index] = packed
        own.append(jnp.stack(rows))

    pl.semaphore_wait(barrier, n_gy - 1 + (n_gx - 1) * columns)

    def start_wait(copies):
        for cond, make in copies:
            guarded(cond, lambda make=make: make().start())

    def wait_recv(copies):
        for cond, make in copies:
            guarded(cond, lambda make=make: make().wait_recv())

    def wait_send(copies):
        for cond, make in copies:
            guarded(cond, lambda make=make: make().wait_send())

    def remote(src, dst, ssem, rsem, x, y):
        return pltpu.make_async_remote_copy(
            src_ref=src, dst_ref=dst, send_sem=ssem, recv_sem=rsem,
            device_id=(x, y), device_id_type=MESH,
        )

    halo_send, halo_recv = [], []
    for dx in (-1, 0, 1):
        for dy in (-1, 0, 1):
            if dx == 0 and dy == 0:
                continue
            conds = [c for c in (ok_gx[dx], ok_gy[dy]) if c is not None]
            cond = conds[0] if len(conds) == 1 else jnp.logical_and(conds[0], conds[1])
            place = 3 * (dx + 1) + dy + 1
            back = 3 * (1 - dx) + 1 - dy

            def views(dx=dx, dy=dy):
                if dy == 0:
                    start = 0 if dx < 0 else 16 - HALO
                    return tile.at[:, pl.ds(start, HALO)], from_rows.at[(1 - dx) // 2]
                if dx == 0:
                    return side, from_side.at[(1 - dy) // 2]
                part = 0 if dx < 0 else 1
                return side.at[part], from_corner.at[(1 - dx) // 2, (1 - dy) // 2]

            def landing(dx=dx, dy=dy):
                if dy == 0:
                    return from_rows.at[(1 + dx) // 2]
                if dx == 0:
                    return from_side.at[(1 + dy) // 2]
                return from_corner.at[(1 + dx) // 2, (1 + dy) // 2]

            def out(views=views, dx=dx, dy=dy, place=place, back=back):
                src, dst = views()
                return remote(src, dst, send_a.at[place], recv_a.at[back], a + dx, b + dy)

            def arrive(landing=landing, dx=dx, dy=dy, place=place):
                return remote(landing(), landing(), send_a.at[place], recv_a.at[place], a + dx, b + dy)

            halo_send.append((cond, out))
            halo_recv.append((cond, arrive))
    start_wait(halo_send)

    def all_to_all(phase, src, dst, rows):
        sends, recvs = [], []
        for d in range(1, n_gy):
            def out(d=d):
                to = lax.rem(b + d, n_gy)
                return remote(
                    src.at[pl.ds(to * rows, rows)], dst.at[pl.ds(b * rows, rows)],
                    send_x.at[phase, d], recv_x.at[phase, d], a, to,
                )

            def arrive(d=d):
                at = lax.rem(b + n_gy - d, n_gy)
                piece = dst.at[pl.ds(at * rows, rows)]
                return remote(piece, piece, send_x.at[phase, d], recv_x.at[phase, d], a, at)

            sends.append((None, out))
            recvs.append((None, arrive))
        start_wait(sends)
        mine = pl.ds(b * rows, rows)
        dst[mine] = src[mine]
        return sends, recvs

    def gather(buffer, ssem, rsem):
        sends, recvs = [], []
        for dy in (0, -1, 1):
            for d in range(n_gx):
                if dy == 0 and d == 0:
                    continue

                def out(d=d, dy=dy):
                    to = lax.rem(a + d, n_gx)
                    return remote(
                        buffer.at[1, a], buffer.at[1 - dy, a],
                        ssem.at[dy + 1, d], rsem.at[1 - dy, d], to, b + dy,
                    )

                def arrive(d=d, dy=dy):
                    at = lax.rem(a + n_gx - d, n_gx)
                    piece = buffer.at[dy + 1, at]
                    return remote(piece, piece, ssem.at[dy + 1, d], rsem.at[dy + 1, d], at, b + dy)

                sends.append((ok_gy[dy], out))
                recvs.append((ok_gy[dy], arrive))
        start_wait(sends)
        return sends, recvs

    loads[3].wait()
    loads[4].wait()
    list_lane = lax.broadcasted_iota(jnp.int32, (1, 128), 1)
    by_row = jnp.zeros((1, 128), jnp.int32)
    by_slot = jnp.full((1, 128), -1, jnp.int32)
    by_from = jnp.zeros((1, 128), jnp.int32)
    for k in range(32):
        slot, row = boxes[0, k], boxes[1, k]
        by_row = jnp.where(list_lane == row, slot, by_row)
        by_slot = jnp.where(list_lane == slot, row, by_slot)
    for j in range(16):
        by_from = jnp.where(list_lane == froms[j], j, by_from)
    lists[0:1] = by_row
    lists[1:2] = by_slot
    lists[2:3] = by_from
    lists[3:8] = jnp.zeros((5, 128), jnp.int32)
    route = pltpu.make_async_copy(lists, routes, load_sem.at[8])
    route.start()

    to_half = table(128, 128, lambda s, d: jnp.where(s // 2 == d % 64, 0.25, 0.0))
    rim_map = table(128, 256, lambda s, d: (
        jnp.where((d < 16) & (s == 64 + d // 2), 1.0, 0.0)
        + jnp.where((d >= 240) & (s == 72 + d % 16 // 2), 1.0, 0.0)
        + jnp.where((d % 16 == 0) & (s == 80 + d // 32), 1.0, 0.0)
        + jnp.where((d % 16 == 15) & (s == 88 + d // 32), 1.0, 0.0)
    ))
    restrict_map = table(256, 128, lambda s, d: jnp.where(s // 32 * 8 + s % 16 // 2 == d % 64, 0.25, 0.0))

    def packed_coarse(values):
        halves = apply_table(pair_rows(values), to_half)
        left = lax.broadcasted_iota(jnp.int32, (4, 8, 128), 2) < 64
        return jnp.where(left, halves[:4], halves[4:])

    coarse_k[1, a, 0] = packed_coarse(own[0])
    coarse_k[1, a, 1] = packed_coarse(own[1])

    for load in loads[5:]:
        load.wait()
    pcond = pcond_ref[...]
    plane = lax.broadcasted_iota(jnp.int32, pcond.shape, 2)
    player = lax.broadcasted_iota(jnp.int32, pcond.shape, 1)
    p_east = jnp.where(plane < 240, 32.0 * (pcond + lanes(pcond, -16)), 0.0)
    p_north = jnp.where(plane % 16 < 15, 32.0 * (pcond + lanes(pcond, -1)), 0.0)
    p_above = jnp.where(player < 7, 0.5 * (pcond + layers(pcond, -1)), 0.0)
    outside = (
        jnp.where((plane < 16) | (plane >= 240), 64.0, 0.0)
        + jnp.where((plane % 16 == 0) | (plane % 16 == 15), 64.0, 0.0)
    )
    p_diag = (
        pcap_ref[...] + outside * pcond + p_east + lanes(p_east, 16)
        + p_north + lanes(p_north, 1) + p_above + layers(p_above, 1)
    )
    p_gain = RELAX / p_diag

    def p_around(values):
        return (
            p_east * lanes(values, -16) + lanes(p_east * values, 16)
            + p_north * lanes(values, -1) + lanes(p_north * values, 1)
            + p_above * layers(values, -1) + layers(p_above * values, 1)
        )

    route.wait()

    wait_recv(halo_recv)
    count = 16 + 2 * HALO
    shape0 = (count, 8, 256)
    row0 = lax.broadcasted_iota(jnp.int32, shape0, 0)
    lane0 = lax.broadcasted_iota(jnp.int32, shape0, 2)
    left_i, right_i = has_left.astype(jnp.int32), has_right.astype(jnp.int32)
    up_i, down_i = has_up.astype(jnp.int32), has_down.astype(jnp.int32)
    inside0 = (
        (row0 >= HALO * (1 - up_i)) & (row0 < 16 + HALO + HALO * down_i)
        & ((lane0 < 128) | ((lane0 < 192) & (right_i > 0)) | ((lane0 >= 192) & (left_i > 0)))
    )
    last8 = lane % 16 < 8
    framed = []
    for index in range(3):
        body = jnp.concatenate([from_rows[0, index], own[index], from_rows[1, index]], axis=0)
        middle = [jnp.where(last8, from_side[0, p, index], from_side[1, p, index]) for p in range(2)]
        upper = jnp.where(last8, from_corner[0, 0, index], from_corner[0, 1, index])
        lower = jnp.where(last8, from_corner[1, 0, index], from_corner[1, 1, index])
        flank = []
        for x in range(-HALO, 16 + HALO):
            source = upper if x < 0 else lower if x >= 16 else middle[x // 8]
            flank.append(lanes(source, -(16 * (x % 8) + 8)))
        body = jnp.concatenate([body, jnp.stack(flank)], axis=2)
        framed.append(jnp.where(inside0, body, 0.0))
    stencil0 = stencil_of(framed[0], framed[1], 16.0, inside0)
    source0 = framed[2]
    u_a = smooth(stencil0[5] * source0, source0, stencil0)

    windows_into(u_a, slots)
    for r in range(32):
        out1[r] = slots[routes[0, r]]
    sends1, recvs1 = all_to_all(0, out1, in1, cap_rows)
    sends_k, recvs_k = gather(coarse_k, send_k, recv_k)
    r_0 = residual_of(u_a, source0, stencil0)[HALO:HALO + 16, :, :128]

    wait_recv(recvs1)
    for j in range(16):
        win1[j] = in1[froms[j]]
    first = win1[...]
    p_rhs = prhs_ref[...]
    p_edge = 64.0 * pcond
    p_source = p_rhs + p_edge * apply_table(first, rim_map)
    v_a = p_gain * p_source
    v_a = (1.0 - RELAX) * v_a + p_gain * (p_source + p_around(v_a))
    rest[...] = apply_table(p_source - p_diag * v_a + p_around(v_a), restrict_map)
    pack = 2 if cap_rows % 2 == 0 else 1
    for r in range(0, 32, pack):
        if pack == 2:
            out2[r // 2] = jnp.where(lane < 64, rest[routes[2, r]], rest[routes[2, r + 1]])
        else:
            out2[r] = rest[routes[2, r]]
    sends2, recvs2 = all_to_all(1, out2, in2, cap_rows // pack)

    wait_recv(recvs_k)
    rows1 = 8 * n_gx

    def spread_tiles(piece):
        left = lax.broadcasted_iota(jnp.int32, (4, 8, 128), 2) < 64
        blocks = []
        for t in range(n_gx):
            low, mid, high = piece(0, t), piece(1, t), piece(2, t)
            low_r, mid_r, high_r = lanes(low, 64), lanes(mid, 64), lanes(high, 64)
            blocks.append(jnp.concatenate([jnp.where(left, mid, high_r), low_r], axis=2))
            blocks.append(jnp.concatenate([jnp.where(left, mid_r, high), low], axis=2))
        return jnp.concatenate(blocks, axis=0)

    def inside_of(rows, width):
        lane_in = lax.broadcasted_iota(jnp.int32, (rows, 8, max(width * 4, 128)), 2)
        part = lane_in // width % 4
        return (part == 0) | ((part == 1) & (right_i > 0)) | ((part == 3) & (left_i > 0))

    halve_1 = table(256, 128, lambda s, d: jnp.where(s // 2 == d, 0.25, 0.0))
    halve_2 = to_half
    widen_3 = table(128, 128, lambda s, d: jnp.where(s == d // 2, 1.0, 0.0))
    widen_2 = table(128, 256, lambda s, d: jnp.where(s == d // 2, 1.0, 0.0))
    widen_1 = table(256, 256, lambda s, d: jnp.where(
        s == d // 2 + jnp.where(d >= 192, 128, 0), 1.0, 0.0))

    inside1 = inside_of(rows1, 64)
    k1 = jnp.where(inside1, spread_tiles(lambda s, t: coarse_k[s, t, 0]), 0.0)
    c1 = jnp.where(inside1, spread_tiles(lambda s, t: coarse_k[s, t, 1]), 0.0)
    k2, c2 = apply_table(pair_rows(k1), halve_1), apply_table(pair_rows(c1), halve_1)
    k3, c3 = apply_table(pair_rows(k2), halve_2), apply_table(pair_rows(c2), halve_2)
    stencil1 = stencil_of(k1, c1, 4.0, inside1)
    stencil2 = stencil_of(k2, c2, 1.0, inside_of(rows1 // 2, 32))
    stencil3 = stencil_of(k3, c3, 0.25, inside_of(rows1 // 4, 16))

    wait_recv(recvs2)
    pieces = []
    for band in range(2):
        items = []
        for col in range(16):
            at = routes[1, 16 * band + col]
            flag = jnp.where(at >= 0, 1.0, 0.0).astype(F32)
            row = jnp.maximum(at, 0)
            item = in2[row // pack]
            if pack == 2:
                item = jnp.where(lane >= 128 * (1 - row % 2), lanes(item, 64), item)
            items.append(jnp.where(lane // 8 == 8, flag, item))
        placed = exchange_groups(items)
        for i in range(8):
            pieces.append(jnp.where(placed[8] > 0.5, placed[i], r_0[8 * band + i]))
    coarse_g[1, a] = packed_coarse(jnp.stack(pieces))
    sends_g, recvs_g = gather(coarse_g, send_g, recv_g)
    wait_recv(recvs_g)

    g1 = jnp.where(inside1, spread_tiles(lambda s, t: coarse_g[s, t]), 0.0)
    e1 = smooth(stencil1[5] * g1, g1, stencil1)
    g2 = apply_table(pair_rows(residual_of(e1, g1, stencil1)), halve_1)
    e2 = smooth(stencil2[5] * g2, g2, stencil2)
    g3 = apply_table(pair_rows(residual_of(e2, g2, stencil2)), halve_2)
    e3 = stencil3[5] * g3
    e3 = lax.fori_loop(0, SWEEPS - 1, lambda _, v: smooth(v, g3, stencil3), e3)
    e2 = smooth(e2 + apply_table(repeat_rows(e3), widen_3), g2, stencil2)
    e1 = smooth(e1 + apply_table(repeat_rows(e2), widen_2), g1, stencil1)
    column[pl.ds(0, 2)] = jnp.zeros((2, 8, 256), F32)
    column[pl.ds(rows1 + 2, 2)] = jnp.zeros((2, 8, 256), F32)
    column[pl.ds(2, rows1)] = e1
    near = column[pl.ds(8 * a, 12)]
    u_b = u_a + jnp.where(inside0, apply_table(repeat_rows(near), widen_1), 0.0)
    solved = smooth(u_b, source0, stencil0)

    windows_into(solved, slots)
    for r in range(32):
        out3[r] = slots[routes[0, r]]
    sends3, recvs3 = all_to_all(2, out3, in3, cap_rows)
    for x in range(16):
        field_ref[pl.ds(x, 8, stride=16), :] = solved[HALO + x, :, :128]
    grow_map = table(128, 256, lambda s, d: jnp.where(s == d // 32 * 8 + d % 16 // 2, 1.0, 0.0))
    wait_recv(recvs3)
    for j in range(16):
        win2[j] = in3[froms[j]]
    second = win2[...]
    values = v_a + apply_table(second - first, grow_map)
    p_source = p_rhs + p_edge * apply_table(second, rim_map)
    patch_ref[...] = (1.0 - RELAX) * values + p_gain * (p_source + p_around(values))

    for copies in (halo_send, sends1, sends_k, sends2, sends_g, sends3):
        wait_send(copies)


def body(n_gx, n_gy, rhs_base, cond_base, cap_base, patch_rhs, patch_cond, patch_cap, box_list, patch_from):
    cap_rows = 2 * patch_rhs.shape[0] // n_gy
    vmem = pl.BlockSpec(memory_space=pltpu.VMEM)
    far = pl.BlockSpec(memory_space=pltpu.HBM)
    dma = pltpu.SemaphoreType.DMA
    buffer = pltpu.VMEM((32, 8, 128), F32)
    field, patches = pl.pallas_call(
        functools.partial(kernel, n_gx, n_gy, cap_rows),
        out_shape=(
            jax.ShapeDtypeStruct((128, 128), F32),
            jax.ShapeDtypeStruct(patch_rhs.shape, F32),
        ),
        in_specs=[far] * 8,
        out_specs=(vmem, vmem),
        scratch_shapes=[
            pltpu.SMEM((2, 32), jnp.int32), pltpu.SMEM((16,), jnp.int32),
            pltpu.VMEM((8, 128), jnp.int32), pltpu.SMEM((8, 128), jnp.int32),
            pltpu.VMEM((128, 128), F32), pltpu.VMEM((128, 128), F32), pltpu.VMEM((128, 128), F32),
            pltpu.VMEM(patch_rhs.shape, F32), pltpu.VMEM(patch_rhs.shape, F32),
            pltpu.VMEM(patch_rhs.shape, F32), dma((9,)),
            pltpu.VMEM((3, 16, 8, 128), F32),
            pltpu.VMEM((2, 3, 8, 128), F32),
            pltpu.VMEM((2, 3, HALO, 8, 128), F32),
            pltpu.VMEM((2, 2, 3, 8, 128), F32),
            pltpu.VMEM((2, 2, 3, 8, 128), F32),
            buffer, buffer, buffer, buffer, buffer, buffer, buffer,
            pltpu.VMEM((16, 8, 128), F32),
            pltpu.VMEM((16, 8, 128), F32),
            pltpu.VMEM((16, 8, 128), F32),
            pltpu.VMEM((3, n_gx, 2, 4, 8, 128), F32),
            pltpu.VMEM((3, n_gx, 4, 8, 128), F32),
            pltpu.VMEM((8 * n_gx + 4, 8, 256), F32),
            dma((9,)), dma((9,)),
            dma((3, n_gy)), dma((3, n_gy)),
            dma((3, n_gx)), dma((3, n_gx)),
            dma((3, n_gx)), dma((3, n_gx)),
        ],
        compiler_params=pltpu.CompilerParams(
            collective_id=0, has_side_effects=True, vmem_limit_bytes=64 * 1024 * 1024
        ),
    )(
        box_list.T, patch_from,
        rhs_base.reshape(128, 128), cond_base.reshape(128, 128), cap_base.reshape(128, 128),
        patch_rhs, patch_cond, patch_cap,
    )
    return field.reshape(rhs_base.shape), patches


def solution(mesh):
    return jax.shard_map(
        functools.partial(body, mesh.shape["gx"], mesh.shape["gy"]),
        mesh=mesh,
        in_specs=(
            P(None, "gx", "gy"),
            P(None, "gx", "gy"),
            P(None, "gx", "gy"),
            P(("gx", "gy"), None, None),
            P(("gx", "gy"), None, None),
            P(("gx", "gy"), None, None),
            P(("gx", "gy"), None),
            P(("gx", "gy")),
        ),
        out_specs=(P(None, "gx", "gy"), P(("gx", "gy"), None, None)),
        check_vma=False,
    )
```
